32 devices in a mesh: scen: 4 (over z), net: 8 (over y, x, core).
Axes of the slice: x: 2, y: 2, z: 4, core: 2. Of those that a mesh axis runs over, the one named last changes fastest.
Arguments:
- coupling: bfloat16 [768, 64, 320], P('net'), may hold values from -0.3125 to 0.3125
- tie_blocks: bfloat16 [1024, 64, 128], P('net'), may hold values from -0.5 to 0.5
- w_pattern: int32 [768, 4], P('net'), may hold values from 0 to 127
- link_pattern: int32 [768], P('net'), may hold values from 0 to 127
- left_bounds: int32 [1024], P('net'), may hold values from 0 to 127
- right_bounds: int32 [1024], P('net'), may hold values from 0 to 127
- block_counts: int32 [8], P('net'), may hold values from 48 to 96, as said below
- commit_cost: float32 [1024, 64], P('net'), may hold values from -3 to 3
- dispatch_cost: float32 [1024, 64], P('net'), may hold values from -6 to 6
- demand: float32 [768, 64], P('net'), may hold values from -6 to 6
- wind_error: bfloat16 [768, 64, 512], P('net', None, 'scen'), may hold values from -3 to 3
- commit_start: float32 [1024, 64], P('net'), may hold values from 0 to 1
- dispatch_start: float32 [1024, 64, 512], P('net', None, 'scen'), may hold values from 0 to 2
- dual_start: float32 [768, 64, 512], P('net', None, 'scen'), may hold values from -8 to 8
- tie_start: float32 [1024, 64, 512], P('net', None, 'scen'), may hold values from -6 to 6
Outputs:
- commit_out: float32 [1024, 64], P('net')
- dispatch_out: float32 [1024, 64, 512], P('net', None, 'scen')
- dual_out: float32 [768, 64, 512], P('net', None, 'scen')
- tie_out: float32 [1024, 64, 512], P('net', None, 'scen')
The draws below stay inside these ranges and needn't reach their ends.
Inputs may be any that keep to these rules, and one draw needn't show every extreme that they name: `block_counts`: some partition has all 96 row blocks active.
All inputs are finite; a program needn't handle non-finite values.
Results may differ from the reference program's by a relative error of at most 0.0035.
Values may be sent and summed in bfloat16 or wider, within the bound.
A program may use at most 192 MiB of HBM per device.

```python
import jax
import jax.numpy as jnp
from jax import lax

BLK = 64
KW = 4
ITERS = 2
YB = 128
RB = 96
XB = 128
BB = 128
PARTS_SIZE = 8
SCEN = 512
NYB = 1024
NRB = 768
NXB = 1024
NBB = 1024


def draw_block_counts(key, part):
    key_a, key_b = jax.random.split(jax.random.fold_in(key, 11))
    drawn = jax.random.randint(key_a, (PARTS_SIZE,), RB // 2, RB + 1)
    fullest = jax.random.randint(key_b, (), 0, PARTS_SIZE)
    return jnp.where(jnp.arange(PARTS_SIZE) == fullest, RB, drawn).astype(jnp.int32)


def draw_dual_start(key, part):
    key_a, key_b = jax.random.split(jax.random.fold_in(key, 23), 2)
    common = jax.random.normal(key_a, (NRB, BLK, 1), jnp.float32)
    values = common + 0.5 * jax.random.normal(key_b, (NRB, BLK, SCEN), jnp.float32)
    return jnp.clip(values, -8.0, 8.0)


def place_ends(array, rng, least, top_value):
    longest = array.shape.index(max(array.shape))
    spots = []
    for shift in (0, 1):
        where = [jax.random.randint(jax.random.fold_in(rng, axis), (), 0, length) for axis, length in enumerate(array.shape)]
        where[longest] = (where[longest] + shift) % array.shape[longest]
        spots.append(tuple(where))
    return array.at[spots[0]].set(least).at[spots[1]].set(top_value)


def steps_of(stream_key, dims, cuts, least, high):
    factor_of, own = 1.0, jax.random.fold_in(stream_key, 6)
    for position, shards_of in cuts:
        draws = jnp.exp(jax.random.uniform(jax.random.fold_in(own, position), (shards_of,), jnp.float32, least / len(cuts), high / len(cuts)))
        factor_of = factor_of * jnp.repeat(draws, dims[position] // shards_of).reshape([-1 if axis == position else 1 for axis in range(len(dims))])
    return factor_of


def normal_values(stream_key, dims, scale, most, shards=(), kind=jnp.bfloat16):
    values = scale * jax.random.normal(stream_key, dims, jnp.float32)
    if shards:
        values = values * steps_of(stream_key, dims, shards, -0.22, 0.18)
    return jnp.clip(values, -most, most).astype(kind)


def setup_inputs(seed: int = 0) -> dict:
    splits = jax.random.split(jax.random.key(seed), 16)
    return {
        "coupling": normal_values(splits[0], (NRB, BLK, (KW + 1) * BLK), ((KW + 1) * BLK) ** -0.5, 0.3125, ((0, 8),)),
        "tie_blocks": normal_values(splits[1], (NBB, BLK, 2 * BLK), (2 * BLK) ** -0.5, 0.5, ((0, 8),)),
        "w_pattern": place_ends(jax.random.randint(splits[2], (NRB, KW), 0, YB), jax.random.fold_in(splits[2], 1), 0, YB - 1).astype(jnp.int32),
        "link_pattern": place_ends(jax.random.randint(splits[3], (NRB,), 0, XB), jax.random.fold_in(splits[3], 1), 0, XB - 1).astype(jnp.int32),
        "left_bounds": place_ends(jax.random.randint(splits[4], (NBB,), 0, YB), jax.random.fold_in(splits[4], 1), 0, YB - 1).astype(jnp.int32),
        "right_bounds": place_ends(jax.random.randint(splits[5], (NBB,), 0, YB), jax.random.fold_in(splits[5], 1), 0, YB - 1).astype(jnp.int32),
        "block_counts": draw_block_counts(jax.random.fold_in(splits[15], 71), 0),
        "commit_cost": normal_values(splits[7], (NXB, BLK), 0.5, 3.0, ((0, 8),), jnp.float32),
        "dispatch_cost": normal_values(splits[8], (NYB, BLK), 1.0, 6.0, ((0, 8),), jnp.float32),
        "demand": normal_values(splits[9], (NRB, BLK), 1.0, 6.0, ((0, 8),), jnp.float32),
        "wind_error": normal_values(splits[10], (NRB, BLK, SCEN), 0.5, 3.0, ((0, 8), (2, 4))),
        "commit_start": jnp.clip(1.0 * jax.random.uniform(splits[11], (NXB, BLK), jnp.float32) ** steps_of(splits[11], (NXB, BLK), ((0, 8),), -0.2, 0.2), 0.0, 1.0),
        "dispatch_start": jnp.clip(2.0 * jax.random.uniform(splits[12], (NYB, BLK, SCEN), jnp.float32) ** steps_of(splits[12], (NYB, BLK, SCEN), ((0, 8), (2, 4)), -0.2, 0.2), 0.0, 2.0),
        "dual_start": draw_dual_start(jax.random.fold_in(splits[15], 71), 0),
        "tie_start": normal_values(splits[14], (NBB, BLK, SCEN), 1.0, 6.0, ((0, 8), (2, 4)), jnp.float32),
    }


def forward_blocks(block_mats, stacked):
    block_count = block_mats.shape[0]
    joined = stacked.astype(jnp.float32).reshape(block_count, -1, stacked.shape[-1])
    return jnp.einsum('roj,rjs->ros', block_mats.astype(jnp.float32), joined)


def backward_blocks(block_mats, dual_rows, width):
    block_count = block_mats.shape[0]
    result = jnp.einsum('roj,ros->rjs', block_mats.astype(jnp.float32), dual_rows.astype(jnp.float32))
    return result.reshape(block_count, width, BLK, -1)


def reference(coupling, tie_blocks, w_pattern, link_pattern, left_bounds, right_bounds, block_counts, commit_cost, dispatch_cost, demand, wind_error, commit_start, dispatch_start, dual_start, tie_start):
    part_count = PARTS_SIZE
    active = (jnp.arange(RB)[None, :] < block_counts[:, None]).astype(jnp.float32).reshape(NRB, 1, 1)
    live_tie = jnp.repeat((jnp.arange(part_count) < part_count - 1).astype(jnp.float32), BB)[:, None, None]
    weight_parts = coupling.reshape(part_count, RB, BLK, (KW + 1) * BLK)
    pattern_parts = w_pattern.reshape(part_count, RB, KW)
    link_parts = link_pattern.reshape(part_count, RB)
    tie_parts = tie_blocks.reshape(part_count, BB, BLK, 2 * BLK)
    left_parts = left_bounds.reshape(part_count, BB)
    right_parts = right_bounds.reshape(part_count, BB)
    cost_col = dispatch_cost[:, :, None]
    target = demand[:, :, None] + wind_error.astype(jnp.float32)
    first_now = commit_start
    second_now = dispatch_start
    dual_now = dual_start * active
    tie_now = tie_start * live_tie
    for iteration in range(ITERS):
        dual_half = dual_now.astype(jnp.bfloat16).reshape(part_count, RB, BLK, -1)
        tie_half = tie_now.astype(jnp.bfloat16).reshape(part_count, BB, BLK, -1)

        def backward_part(inputs):
            weight_p, pattern_p, link_p, dual_p = inputs
            block_terms = backward_blocks(weight_p, dual_p, KW + 1)
            grad_second = jax.ops.segment_sum(block_terms[:, :KW].reshape(RB * KW, BLK, -1), pattern_p.reshape(-1), num_segments=YB)
            link_terms = jnp.sum(block_terms[:, KW], axis=2) / SCEN
            grad_first = jax.ops.segment_sum(link_terms, link_p, num_segments=XB)
            return grad_second, grad_first

        grad_second, grad_first = lax.map(backward_part, (weight_parts, pattern_parts, link_parts, dual_half))
        tie_terms = jax.vmap(lambda mats_p, duals_p: backward_blocks(mats_p, duals_p, 2))(tie_parts, tie_half)
        own_terms = tie_terms[:, :, 0]
        left_terms = tie_terms[:, :, 1]
        left_terms = jnp.concatenate([jnp.zeros_like(left_terms[:1]), left_terms[:-1]], axis=0)
        add_own = jax.vmap(lambda vals, idx: jax.ops.segment_sum(vals, idx, num_segments=YB))(own_terms, right_parts)
        add_left = jax.vmap(lambda vals, idx: jax.ops.segment_sum(vals, idx, num_segments=YB))(left_terms, left_parts)
        grad_second = (grad_second + add_own + add_left).reshape(NYB, BLK, -1)
        grad_first = grad_first.reshape(NXB, BLK)
        first_next = jnp.clip(first_now - 1.0 * (commit_cost - grad_first), 0.0, 1.0)
        second_next = jnp.maximum(second_now - 0.4 * (cost_col - grad_second), 0.0)
        first_bar = (2.0 * first_next - first_now).astype(jnp.bfloat16).reshape(part_count, XB, BLK)
        second_bar = (2.0 * second_next - second_now).astype(jnp.bfloat16).reshape(part_count, YB, BLK, -1)

        def forward_part(inputs):
            weight_p, pattern_p, link_p, second_p, first_p = inputs
            gathered = second_p[pattern_p]
            linked = jnp.broadcast_to(first_p[link_p][:, None, :, None], (RB, 1, BLK, gathered.shape[3]))
            return forward_blocks(weight_p, jnp.concatenate([gathered, linked], axis=1))

        coupled = lax.map(forward_part, (weight_parts, pattern_parts, link_parts, second_bar, first_bar)).reshape(NRB, BLK, -1)
        own_rows = jax.vmap(lambda vals, idx: vals[idx])(second_bar, right_parts)
        next_rows = jax.vmap(lambda vals, idx: vals[idx])(second_bar, left_parts)
        next_rows = jnp.concatenate([next_rows[1:], jnp.zeros_like(next_rows[:1])], axis=0)
        tie_inputs = jnp.stack([own_rows, next_rows], axis=2)
        tie_rows = jax.vmap(forward_blocks)(tie_parts, tie_inputs).reshape(NBB, BLK, -1)
        dual_now = (dual_now + 0.4 * (target - coupled)) * active
        tie_now = (tie_now - 0.4 * tie_rows) * live_tie
        first_now = first_next
        second_now = second_next
    return first_now, second_now, dual_now, tie_now
```

```python
import functools

import jax
import jax.numpy as jnp
from jax import lax
from jax.experimental import pallas as pl
from jax.experimental.pallas import tpu as pltpu
from jax.sharding import PartitionSpec as P

BLK = 64
KW = 4
ITERS = 2
CHUNKS = 8
UNROLL = 16

primal_step = 0.4
first_step = 1.0
dual_step = 0.4

F32 = jnp.float32
BF16 = jnp.bfloat16
MESH = pl.DeviceIdType.MESH


def transposed_dot(a, b):
    return lax.dot_general(a, b, (((0,), (0,)), ((), ())), preferred_element_type=F32)


def spread(columns, at):
    return jnp.broadcast_to(columns[:, at : at + 1], columns.shape)


def loop(count, step, carry=0, unroll=UNROLL):
    unroll = max(u for u in range(1, unroll + 1) if count % u == 0)
    return lax.fori_loop(0, count // unroll, lambda c, state: step(c * unroll, unroll, state), carry)


def layout_of(rows, ties, blocks, slots):
    sizes = dict(
        count=1,
        pattern=rows * KW,
        link=rows,
        prev_rec=KW * rows,
        last_rec=KW * blocks,
        right=ties,
        prev_own=ties,
        last_own=blocks,
        prev_out=ties,
        last_out=slots,
        slot_of_tie=ties,
        slot_of_block=blocks,
        block_of_slot=slots,
    )
    offsets, at = {}, 0
    for name, size in sizes.items():
        offsets[name] = at
        at += size
    return offsets


def kernel(
    offsets,
    index,
    cost_t,
    demand_t,
    commit_cost_t,
    commit_t,
    coupling_hbm,
    tie_hbm,
    wind_hbm,
    second_hbm,
    lam_hbm,
    mu_hbm,
    commit_out,
    second_out,
    lam_out,
    mu_out,
    coupling,
    tie,
    wind,
    second,
    lam,
    mu,
    rec0,
    rec1,
    rec2,
    rec3,
    outs,
    own,
    send_terms,
    got_terms0,
    got_terms1,
    send_bar,
    got_bar0,
    got_bar1,
    bar,
    first_wide,
    first_t,
    send_first,
    got_first,
    load_sems,
    store_sems,
    terms_ssem,
    terms_rsem,
    bar_ssem,
    bar_rsem,
    first_ssem,
    first_rsem,
):
    recs = (rec0, rec1, rec2, rec3)
    got_terms, got_bar = (got_terms0, got_terms1), (got_bar0, got_bar1)
    me_s, me = lax.axis_index("scen"), lax.axis_index("net")
    scens, parts = lax.axis_size("scen"), lax.axis_size("net")
    rows, ties, blocks = lam.shape[0], mu.shape[0], second.shape[0]
    slots = send_terms.shape[0]
    scen_total = lam.shape[2] * scens
    has_next, has_prev = me < parts - 1, me > 0

    def at(name, i):
        return index[offsets[name] + i]

    loads = [
        pltpu.make_async_copy(src, dst, load_sems.at[i])
        for i, (src, dst) in enumerate(
            [(tie_hbm, tie), (mu_hbm, mu), (coupling_hbm, coupling), (lam_hbm, lam), (second_hbm, second), (wind_hbm, wind)]
        )
    ]
    for copy in loads:
        copy.start()

    entry = pltpu.get_barrier_semaphore()
    for by in range(1, scens):
        pl.semaphore_signal(entry, inc=1, device_id=(lax.rem(me_s + by, scens), me), device_id_type=MESH)

    @pl.when(has_next)
    def _():
        pl.semaphore_signal(entry, inc=1, device_id=(me_s, me + 1), device_id_type=MESH)

    @pl.when(has_prev)
    def _():
        pl.semaphore_signal(entry, inc=1, device_id=(me_s, me - 1), device_id_type=MESH)

    zero = jnp.zeros(second.shape[1:], F32)
    for ref in recs:
        ref[rows] = zero
    outs[ties] = zero
    own[ties] = zero
    for iteration in range(ITERS):
        got_terms[iteration][slots] = zero.astype(BF16)
    first_t[...] = commit_t[...]

    @pl.when(jnp.logical_not(has_prev))
    def _():
        for iteration in range(ITERS):
            got_terms[iteration][pl.ds(0, slots)] = jnp.zeros((slots,) + second.shape[1:], BF16)

    @pl.when(jnp.logical_not(has_next))
    def _():
        for iteration in range(ITERS):
            got_bar[iteration][...] = jnp.zeros((slots,) + second.shape[1:], BF16)

    pl.semaphore_wait(entry, scens - 1 + has_next.astype(jnp.int32) + has_prev.astype(jnp.int32))

    lanes = lax.broadcasted_iota(jnp.int32, second.shape[1:], 1)
    span = slots // CHUNKS

    def terms_copy(iteration, c):
        return pltpu.make_async_remote_copy(
            src_ref=send_terms.at[pl.ds(c * span, span)],
            dst_ref=got_terms[iteration].at[pl.ds(c * span, span)],
            send_sem=terms_ssem.at[iteration, c],
            recv_sem=terms_rsem.at[iteration, c],
            device_id=(me_s, me + 1),
            device_id_type=MESH,
        )

    def bar_copy(iteration, c):
        return pltpu.make_async_remote_copy(
            src_ref=send_bar.at[pl.ds(c * span, span)],
            dst_ref=got_bar[iteration].at[pl.ds(c * span, span)],
            send_sem=bar_ssem.at[iteration, c],
            recv_sem=bar_rsem.at[iteration, c],
            device_id=(me_s, me - 1),
            device_id_type=MESH,
        )

    def first_copy(iteration, by):
        return pltpu.make_async_remote_copy(
            src_ref=send_first.at[iteration],
            dst_ref=got_first.at[iteration, by],
            send_sem=first_ssem.at[iteration, by],
            recv_sem=first_rsem.at[iteration, by],
            device_id=(lax.rem(me_s + by, scens), me),
            device_id_type=MESH,
        )

    def chain_ties(base, count, news):
        parts_of = [transposed_dot(tie[base + u], news[u].astype(BF16)) for u in range(count)]
        for u in range(count):
            j = base + u
            own[j] = parts_of[u][:BLK] + own[at("prev_own", j)]
            outs[j] = parts_of[u][BLK:] + outs[at("prev_out", j)]

    def start_ties(base, count, carry):
        news = [jnp.where(has_next, mu[base + u], 0.0) for u in range(count)]
        for u in range(count):
            mu[base + u] = news[u]
        chain_ties(base, count, news)
        return carry

    def next_ties(iteration, more):
        def step(base, count, carry):
            news = []
            for u in range(count):
                j = base + u
                stacked = jnp.concatenate([bar[at("right", j)], got_bar[iteration][at("slot_of_tie", j)]], axis=0)
                product = jnp.dot(tie[j], stacked, preferred_element_type=F32)
                news.append(jnp.where(has_next, mu[j] - dual_step * product, 0.0))
            for u in range(count):
                mu[base + u] = news[u]
            if more:
                chain_ties(base, count, news)
            return carry

        loop(ties, step)

    def send_all_terms(iteration):
        def chunk(c, carry):
            def step(base, count, inner):
                blocks_of = [outs[at("last_out", c * span + base + u)] for u in range(count)]
                for u in range(count):
                    send_terms[c * span + base + u] = blocks_of[u].astype(BF16)
                return inner

            loop(span, step)

            @pl.when(has_next)
            def _():
                terms_copy(iteration, c).start()

            return carry

        lax.fori_loop(0, CHUNKS, chunk, 0)

    def chain_rows(base, count, halves, total):
        parts_of = [transposed_dot(coupling[base + u], halves[u]) for u in range(count)]
        for u in range(count):
            r = base + u
            for k in range(KW):
                recs[k][r] = parts_of[u][k * BLK : (k + 1) * BLK] + recs[k][at("prev_rec", k * rows + r)]
            summed = jnp.sum(parts_of[u][KW * BLK :], axis=1, keepdims=True)
            total = total + jnp.where(lanes == at("link", r), summed, 0.0)
        return total

    def start_rows(base, count, total):
        news = [jnp.where(base + u < at("count", 0), lam[base + u], 0.0) for u in range(count)]
        for u in range(count):
            lam[base + u] = news[u]
        return chain_rows(base, count, [new.astype(BF16) for new in news], total)

    def next_rows(more):
        def step(base, count, state):
            total, demand = state
            news = []
            for u in range(count):
                r = base + u
                gathered = [bar[at("pattern", r * KW + k)] for k in range(KW)] + [first_wide[at("link", r)]]
                coupled = jnp.dot(coupling[r], jnp.concatenate(gathered, axis=0), preferred_element_type=F32)
                target = spread(demand, u) + wind[r].astype(F32)
                new = lam[r] + dual_step * (target - coupled)
                news.append(jnp.where(r < at("count", 0), new, 0.0))
            for u in range(count):
                lam[base + u] = news[u]
            if more:
                total = chain_rows(base, count, [new.astype(BF16) for new in news], total)
            return total, pltpu.roll(demand, demand.shape[1] - count, 1)

        return loop(rows, step, (zero, demand_t[...]))[0]

    def send_first_sum(iteration, total):
        send_first[iteration] = (total / scen_total).astype(BF16)
        for by in range(1, scens):
            first_copy(iteration, by).start()

    def move_first(iteration):
        total = send_first[iteration].astype(F32)
        for by in range(1, scens):
            first_copy(iteration, by).wait()
            total = total + got_first[iteration, by].astype(F32)
        now = first_t[...]
        new = jnp.clip(now - first_step * (commit_cost_t[...] - total), 0.0, 1.0)
        first_t[...] = new
        extrapolated = 2.0 * new - now

        def step(base, count, columns):
            for u in range(count):
                first_wide[base + u] = spread(columns, u).astype(BF16)
            return pltpu.roll(columns, columns.shape[1] - count, 1)

        loop(blocks, step, extrapolated)

    def gather_local(base, count, cost):
        moved = []
        for u in range(count):
            b = base + u
            grad = own[at("last_own", b)]
            for k in range(KW):
                grad = grad + recs[k][at("last_rec", k * blocks + b)]
            moved.append(second[b] - primal_step * (spread(cost, u) - grad))
        for u in range(count):
            outs[base + u] = moved[u]
        return pltpu.roll(cost, cost.shape[1] - count, 1)

    def answer_terms(iteration):
        def chunk(c, carry):
            @pl.when(has_prev)
            def _():
                terms_copy(iteration, c).wait_recv()

                def step(base, count, inner):
                    bars = []
                    for u in range(count):
                        d = c * span + base + u
                        b = at("block_of_slot", d)
                        new = jnp.maximum(outs[b] + primal_step * got_terms[iteration][d].astype(F32), 0.0)
                        bars.append((2.0 * new - second[b]).astype(BF16))
                    for u in range(count):
                        send_bar[c * span + base + u] = bars[u]
                    return inner

                loop(span, step)
                bar_copy(iteration, c).start()

            return carry

        lax.fori_loop(0, CHUNKS, chunk, 0)

    def move_second(iteration):
        def step(base, count, carry):
            news = []
            for u in range(count):
                b = base + u
                terms = got_terms[iteration][at("slot_of_block", b)].astype(F32)
                new = jnp.maximum(outs[b] + primal_step * terms, 0.0)
                news.append((new, (2.0 * new - second[b]).astype(BF16)))
            for u in range(count):
                second[base + u], bar[base + u] = news[u]
            return carry

        loop(blocks, step)

    def finish_sends(copy, iteration):
        def chunk(c, carry):
            copy(iteration, c).wait_send()
            return carry

        lax.fori_loop(0, CHUNKS, chunk, 0)

    def finish_receives(copy, iteration):
        def chunk(c, carry):
            copy(iteration, c).wait_recv()
            return carry

        lax.fori_loop(0, CHUNKS, chunk, 0)

    loads[0].wait()
    loads[1].wait()
    loop(ties, start_ties)
    send_all_terms(0)
    loads[2].wait()
    loads[3].wait()
    total = loop(rows, start_rows, zero)
    send_first_sum(0, total)
    loads[4].wait()
    for iteration in range(ITERS):
        more = iteration < ITERS - 1
        loop(blocks, gather_local, cost_t[...])
        answer_terms(iteration)
        move_second(iteration)
        move_first(iteration)
        if iteration == 0:
            loads[5].wait()
        if not more:
            commit_out[...] = first_t[...]
            store_second = pltpu.make_async_copy(second, second_out, store_sems.at[0])
            store_second.start()
        total = next_rows(more)
        if more:
            send_first_sum(iteration + 1, total)
        else:
            store_lam = pltpu.make_async_copy(lam, lam_out, store_sems.at[1])
            store_lam.start()

        @pl.when(has_next)
        def _():
            finish_sends(terms_copy, iteration)
            finish_receives(bar_copy, iteration)

        next_ties(iteration, more)
        if more:
            send_all_terms(iteration + 1)

        @pl.when(has_prev)
        def _():
            finish_sends(bar_copy, iteration)

    store_mu = pltpu.make_async_copy(mu, mu_out, store_sems.at[2])
    store_mu.start()
    store_second.wait()
    store_lam.wait()
    store_mu.wait()


def previous_equal(keys):
    n = keys.shape[-1]
    u = lax.iota(jnp.int32, n)
    same = (keys[..., :, None] == keys[..., None, :]) & (u[None, :] < u[:, None])
    found = jnp.max(jnp.where(same, u[None, :], -1), axis=-1)
    return jnp.where(found < 0, n, found)


def last_equal(keys, wanted):
    n = keys.shape[-1]
    u = lax.iota(jnp.int32, n)
    found = jnp.max(jnp.where(keys[..., None, :] == wanted[:, None], u, -1), axis=-1)
    return jnp.where(found < 0, n, found)


def slot_table(bounds, blocks, slots):
    b = lax.iota(jnp.int32, blocks)
    present = jnp.any(bounds[None, :] == b[:, None], axis=1)
    before = jnp.sum((present[None, :] & (b[None, :] < b[:, None])).astype(jnp.int32), axis=1)
    d = lax.iota(jnp.int32, slots)
    chosen = present[None, :] & (before[None, :] == d[:, None])
    block_of_slot = jnp.sum(jnp.where(chosen, b[None, :], 0), axis=1)
    used = jnp.any(chosen, axis=1)
    return present, before, block_of_slot, used


def body(
    coupling,
    tie_blocks,
    w_pattern,
    link_pattern,
    left_bounds,
    right_bounds,
    block_counts,
    commit_cost,
    dispatch_cost,
    demand,
    wind_error,
    commit_start,
    dispatch_start,
    dual_start,
    tie_start,
):
    parts = lax.axis_size("net")
    scens = lax.axis_size("scen")
    rows, ties, blocks = dual_start.shape[0], tie_start.shape[0], dispatch_start.shape[0]
    block_shape = dispatch_start.shape[1:]
    slots = blocks
    left_next = lax.ppermute(left_bounds, "net", [(i + 1, i) for i in range(parts - 1)])
    b = lax.iota(jnp.int32, blocks)
    keys = w_pattern.T
    present, before, block_of_slot, _ = slot_table(left_bounds, blocks, slots)
    present_next, before_next, block_next, used_next = slot_table(left_next, blocks, slots)
    slot_of_tie = jnp.sum((present_next[None, :] & (b[None, :] < left_next[:, None])).astype(jnp.int32), axis=1)
    last_out = jnp.where(used_next, last_equal(left_next, block_next), ties)
    offsets = layout_of(rows, ties, blocks, slots)
    index = jnp.concatenate(
        [
            block_counts,
            w_pattern.reshape(-1),
            link_pattern,
            previous_equal(keys).reshape(-1),
            last_equal(keys, b).reshape(-1),
            right_bounds,
            previous_equal(right_bounds),
            last_equal(right_bounds, b),
            previous_equal(left_next),
            last_out,
            slot_of_tie,
            jnp.where(present, before, slots),
            block_of_slot,
        ]
    )
    lanes = block_shape[1]

    def turned(value):
        return jnp.pad(value.T, ((0, 0), (0, lanes - value.shape[0])))

    vmem = pl.BlockSpec(memory_space=pltpu.VMEM)
    anywhere = pl.BlockSpec(memory_space=pl.ANY)
    wide = lambda count, kind: pltpu.VMEM((count,) + block_shape, kind)
    sems = pltpu.SemaphoreType.DMA
    commit_t, second, lam, mu = pl.pallas_call(
        functools.partial(kernel, offsets),
        out_shape=(
            jax.ShapeDtypeStruct((BLK, blocks), F32),
            jax.ShapeDtypeStruct(dispatch_start.shape, F32),
            jax.ShapeDtypeStruct(dual_start.shape, F32),
            jax.ShapeDtypeStruct(tie_start.shape, F32),
        ),
        in_specs=[pl.BlockSpec(memory_space=pltpu.SMEM)] + [vmem] * 4 + [anywhere] * 6,
        out_specs=(vmem, anywhere, anywhere, anywhere),
        scratch_shapes=[
            pltpu.VMEM(coupling.shape, BF16),
            pltpu.VMEM(tie_blocks.shape, BF16),
            pltpu.VMEM(wind_error.shape, BF16),
            wide(blocks, F32),
            wide(rows, F32),
            wide(ties, F32),
            wide(rows + 1, F32),
            wide(rows + 1, F32),
            wide(rows + 1, F32),
            wide(rows + 1, F32),
            wide(ties + 1, F32),
            wide(ties + 1, F32),
            wide(slots, BF16),
            wide(slots + 1, BF16),
            wide(slots + 1, BF16),
            wide(slots, BF16),
            wide(slots, BF16),
            wide(slots, BF16),
            wide(blocks, BF16),
            wide(blocks, BF16),
            pltpu.VMEM(block_shape, F32),
            pltpu.VMEM((ITERS,) + block_shape, BF16),
            pltpu.VMEM((ITERS, scens) + block_shape, BF16),
            sems((6,)),
            sems((3,)),
            sems((ITERS, CHUNKS)),
            sems((ITERS, CHUNKS)),
            sems((ITERS, CHUNKS)),
            sems((ITERS, CHUNKS)),
            sems((ITERS, scens)),
            sems((ITERS, scens)),
        ],
        compiler_params=pltpu.CompilerParams(
            collective_id=0, has_side_effects=True, vmem_limit_bytes=62 * 2**20
        ),
        cost_estimate=pl.CostEstimate(flops=32 * 10**8, bytes_accessed=30 * 10**6, transcendentals=0),
    )(
        index,
        turned(dispatch_cost),
        turned(demand),
        turned(commit_cost),
        turned(commit_start),
        coupling,
        tie_blocks,
        wind_error,
        dispatch_start,
        dual_start,
        tie_start,
    )
    return commit_t.T[: commit_start.shape[0]], second, lam, mu


def solution(mesh):
    return jax.shard_map(
        body,
        mesh=mesh,
        in_specs=(
            P("net", None, None),
            P("net", None, None),
            P("net", None),
            P("net"),
            P("net"),
            P("net"),
            P("net"),
            P("net", None),
            P("net", None),
            P("net", None),
            P("net", None, "scen"),
            P("net", None),
            P("net", None, "scen"),
            P("net", None, "scen"),
            P("net", None, "scen"),
        ),
        out_specs=(
            P("net", None),
            P("net", None, "scen"),
            P("net", None, "scen"),
            P("net", None, "scen"),
        ),
        check_vma=False,
    )
```

```python
import functools

import jax
import jax.numpy as jnp
from jax import lax
from jax.experimental import pallas as pl
from jax.experimental.pallas import tpu as pltpu
from jax.sharding import PartitionSpec as P

BLK = 64
KW = 4
ITERS = 2
CHUNKS = 8
UNROLL = 16

primal_step = 0.4
first_step = 1.0
dual_step = 0.4

F32 = jnp.float32
BF16 = jnp.bfloat16
MESH = pl.DeviceIdType.MESH


def transposed_dot(a, b):
    return lax.dot_general(a, b, (((0,), (0,)), ((), ())), preferred_element_type=F32)


def spread(columns, at):
    return jnp.broadcast_to(columns[:, at : at + 1], columns.shape)


def loop(count, step, carry=0, unroll=UNROLL):
    unroll = max(u for u in range(1, unroll + 1) if count % u == 0)
    return lax.fori_loop(0, count // unroll, lambda c, state: step(c * unroll, unroll, state), carry)


TABLE = dict(
    pattern=0,
    link=4,
    prev_rec=5,
    last_rec=9,
    right=13,
    prev_own=14,
    last_own=15,
    prev_out=16,
    last_out=17,
    slot_of_tie=18,
    slot_of_block=19,
    block_of_slot=20,
    most=21,
    count=22,
)
TABLE_ROWS = 24


def prepare(slots_few, left, right, pattern, link, count, table, most, message, padded, inbox, send_sems, recv_sems):
    me_s, me = lax.axis_index("scen"), lax.axis_index("net")
    parts = lax.axis_size("net")
    lanes = table.shape[1]
    blocks = lanes

    entry = pltpu.get_barrier_semaphore()
    for by in range(1, parts):
        pl.semaphore_signal(entry, inc=1, device_id=(me_s, lax.rem(me + by, parts)), device_id_type=MESH)

    down = lax.broadcasted_iota(jnp.int32, (lanes, lanes), 0)
    along = lax.broadcasted_iota(jnp.int32, (lanes, lanes), 1)

    def both(row):
        spread_row = jnp.broadcast_to(row, (lanes, lanes)).astype(F32)
        return spread_row, spread_row.T

    def most_of(mask, values):
        return jnp.max(jnp.where(mask, values.astype(F32), -1.0), axis=0, keepdims=True)

    def or_else(found, other):
        return jnp.where(found < 0.0, jnp.float32(other), found).astype(jnp.int32)

    def chain(row, n):
        at_lane, at_row = both(row)
        previous = most_of((at_lane == at_row) & (down < along) & (down < n), down)
        last = most_of((at_row == along.astype(F32)) & (down < n), down)
        return previous, last

    def slots_of(row):
        at_lane, at_row = both(row)
        hit = at_row == along.astype(F32)
        present = jnp.max(jnp.where(hit, 1.0, 0.0), axis=0, keepdims=True)
        present_wide = jnp.broadcast_to(present, (lanes, lanes))
        present_down = present_wide.T
        before = jnp.sum(jnp.where(down < along, present_down, 0.0), axis=0, keepdims=True)
        _, before_down = both(before)
        chosen = (present_down > 0.0) & (before_down == along.astype(F32))
        block_of_slot = most_of(chosen, down)
        return present, before, block_of_slot, jnp.sum(present, axis=1, keepdims=True)

    present, before, block_of_slot, count_of = slots_of(left[...])
    message[...] = jnp.zeros(message.shape, jnp.int32)
    message[0:1] = left[...]
    counted = jnp.broadcast_to(count_of, (1, lanes)).astype(jnp.int32)
    message[1:2] = jnp.where(me > 0, counted, 0)
    pl.semaphore_wait(entry, parts - 1)

    def copy(by):
        return pltpu.make_async_remote_copy(
            src_ref=message,
            dst_ref=inbox.at[by],
            send_sem=send_sems.at[by],
            recv_sem=recv_sems.at[by],
            device_id=(me_s, lax.rem(me + by, parts)),
            device_id_type=MESH,
        )

    for by in range(1, parts):
        copy(by).start()

    rows, ties = pattern.shape[1], right.shape[1]
    table[...] = jnp.zeros(table.shape, jnp.int32)
    sentinel = jnp.zeros((1, lanes), jnp.int32) + lanes
    for k in range(KW):
        padded[...] = sentinel
        padded[:, 0:rows] = pattern[k : k + 1]
        row = padded[...]
        table[TABLE["pattern"] + k : TABLE["pattern"] + k + 1] = row
        previous, last = chain(row, rows)
        table[TABLE["prev_rec"] + k : TABLE["prev_rec"] + k + 1] = or_else(previous, rows)
        table[TABLE["last_rec"] + k : TABLE["last_rec"] + k + 1] = or_else(last, rows)
    table[TABLE["link"] : TABLE["link"] + 1, 0:rows] = link[...]
    previous, last = chain(right[...], ties)
    table[TABLE["right"] : TABLE["right"] + 1] = right[...]
    table[TABLE["prev_own"] : TABLE["prev_own"] + 1] = or_else(previous, ties)
    table[TABLE["last_own"] : TABLE["last_own"] + 1] = or_else(last, ties)
    table[TABLE["slot_of_block"] : TABLE["slot_of_block"] + 1] = jnp.where(present > 0.0, before + 1.0, 0.0).astype(jnp.int32)
    table[TABLE["block_of_slot"] : TABLE["block_of_slot"] + 1] = or_else(block_of_slot, 0)
    table[TABLE["count"] : TABLE["count"] + 1] = jnp.zeros((1, lanes), jnp.int32) + count[0]

    highest = message[1:2]
    for by in range(1, parts):
        copy(by).wait()
        highest = jnp.maximum(highest, inbox[by, 1:2])
    most[...] = jnp.where(highest > slots_few, 1, 0)
    left_next = inbox[parts - 1, 0:1]
    previous, last = chain(left_next, ties)
    present, before, block_of_slot, _ = slots_of(left_next)
    at_lane, at_row = both(left_next)
    _, last_down = both(last)
    _, before_down = both(before)
    slot_of_tie = most_of(at_lane == down.astype(F32), before_down)
    _, block_down = both(block_of_slot)
    block_lane, _ = both(block_of_slot)
    last_out = most_of(block_lane == down.astype(F32), last_down)
    table[TABLE["prev_out"] : TABLE["prev_out"] + 1] = or_else(previous, ties)
    table[TABLE["last_out"] : TABLE["last_out"] + 1] = or_else(last_out, ties)
    table[TABLE["slot_of_tie"] : TABLE["slot_of_tie"] + 1] = slot_of_tie.astype(jnp.int32)


def kernel(
    index,
    cost_t,
    demand_t,
    commit_cost_t,
    commit_t,
    coupling_hbm,
    tie_hbm,
    wind_hbm,
    second_hbm,
    lam_hbm,
    mu_hbm,
    commit_out,
    second_out,
    lam_out,
    mu_out,
    coupling,
    tie,
    wind,
    second,
    lam,
    mu,
    rec0,
    rec1,
    rec2,
    rec3,
    outs,
    own,
    send_terms,
    got_terms0,
    got_terms1,
    send_bar,
    got_bar0,
    got_bar1,
    bar,
    first_wide,
    first_t,
    demand_wide,
    send_first,
    got_first,
    load_sems,
    store_sems,
    terms_ssem,
    terms_rsem,
    bar_ssem,
    bar_rsem,
    first_ssem,
    first_rsem,
):
    recs = (rec0, rec1, rec2, rec3)
    got_terms, got_bar = (got_terms0, got_terms1), (got_bar0, got_bar1)
    me_s, me = lax.axis_index("scen"), lax.axis_index("net")
    scens, parts = lax.axis_size("scen"), lax.axis_size("net")
    rows, ties, blocks = lam.shape[0], mu.shape[0], second.shape[0]
    slots = send_terms.shape[0]
    scen_total = lam.shape[2] * scens
    has_next, has_prev = me < parts - 1, me > 0

    def at(name, i, k=0):
        return index[TABLE[name] + k, i]

    loads = [
        pltpu.make_async_copy(src, dst, load_sems.at[i])
        for i, (src, dst) in enumerate(
            [(tie_hbm, tie), (mu_hbm, mu), (coupling_hbm, coupling), (lam_hbm, lam), (second_hbm, second), (wind_hbm, wind)]
        )
    ]
    for copy in loads:
        copy.start()

    entry = pltpu.get_barrier_semaphore()
    for by in range(1, scens):
        pl.semaphore_signal(entry, inc=1, device_id=(lax.rem(me_s + by, scens), me), device_id_type=MESH)

    @pl.when(has_next)
    def _():
        pl.semaphore_signal(entry, inc=1, device_id=(me_s, me + 1), device_id_type=MESH)

    @pl.when(has_prev)
    def _():
        pl.semaphore_signal(entry, inc=1, device_id=(me_s, me - 1), device_id_type=MESH)

    zero = jnp.zeros(second.shape[1:], F32)
    for ref in recs:
        ref[rows] = zero
    outs[ties] = zero
    own[ties] = zero
    for iteration in range(ITERS):
        got_terms[iteration][0] = zero.astype(BF16)
    first_t[...] = commit_t[...]
    demand_wide[:, 0:rows] = demand_t[...]

    @pl.when(jnp.logical_not(has_prev))
    def _():
        for iteration in range(ITERS):
            got_terms[iteration][pl.ds(1, slots)] = jnp.zeros((slots,) + second.shape[1:], BF16)

    @pl.when(jnp.logical_not(has_next))
    def _():
        for iteration in range(ITERS):
            got_bar[iteration][...] = jnp.zeros((slots,) + second.shape[1:], BF16)

    pl.semaphore_wait(entry, scens - 1 + has_next.astype(jnp.int32) + has_prev.astype(jnp.int32))

    lanes = lax.broadcasted_iota(jnp.int32, second.shape[1:], 1)
    span = slots // CHUNKS

    def terms_copy(iteration, c):
        return pltpu.make_async_remote_copy(
            src_ref=send_terms.at[pl.ds(c * span, span)],
            dst_ref=got_terms[iteration].at[pl.ds(1 + c * span, span)],
            send_sem=terms_ssem.at[iteration, c],
            recv_sem=terms_rsem.at[iteration, c],
            device_id=(me_s, me + 1),
            device_id_type=MESH,
        )

    def bar_copy(iteration, c):
        return pltpu.make_async_remote_copy(
            src_ref=send_bar.at[pl.ds(c * span, span)],
            dst_ref=got_bar[iteration].at[pl.ds(c * span, span)],
            send_sem=bar_ssem.at[iteration, c],
            recv_sem=bar_rsem.at[iteration, c],
            device_id=(me_s, me - 1),
            device_id_type=MESH,
        )

    def first_copy(iteration, by):
        return pltpu.make_async_remote_copy(
            src_ref=send_first.at[iteration],
            dst_ref=got_first.at[iteration, by],
            send_sem=first_ssem.at[iteration, by],
            recv_sem=first_rsem.at[iteration, by],
            device_id=(lax.rem(me_s + by, scens), me),
            device_id_type=MESH,
        )

    def chain_ties(base, count, news):
        parts_of = [transposed_dot(tie[base + u], news[u].astype(BF16)) for u in range(count)]
        for u in range(count):
            j = base + u
            own[j] = parts_of[u][:BLK] + own[at("prev_own", j)]
            outs[j] = parts_of[u][BLK:] + outs[at("prev_out", j)]

    def start_ties(base, count, carry):
        news = [jnp.where(has_next, mu[base + u], 0.0) for u in range(count)]
        for u in range(count):
            mu[base + u] = news[u]
        chain_ties(base, count, news)
        return carry

    def next_ties(iteration, more):
        def step(base, count, carry):
            news = []
            for u in range(count):
                j = base + u
                stacked = jnp.concatenate([bar[at("right", j)], got_bar[iteration][at("slot_of_tie", j)]], axis=0)
                product = jnp.dot(tie[j], stacked, preferred_element_type=F32)
                news.append(jnp.where(has_next, mu[j] - dual_step * product, 0.0))
            for u in range(count):
                mu[base + u] = news[u]
            if more:
                chain_ties(base, count, news)
            return carry

        loop(ties, step)

    def send_all_terms(iteration):
        def chunk(c, carry):
            def step(base, count, inner):
                blocks_of = [outs[at("last_out", c * span + base + u)] for u in range(count)]
                for u in range(count):
                    send_terms[c * span + base + u] = blocks_of[u].astype(BF16)
                return inner

            loop(span, step)

            @pl.when(has_next)
            def _():
                terms_copy(iteration, c).start()

            return carry

        lax.fori_loop(0, CHUNKS, chunk, 0)

    def chain_rows(base, count, halves, total):
        parts_of = [transposed_dot(coupling[base + u], halves[u]) for u in range(count)]
        for u in range(count):
            r = base + u
            for k in range(KW):
                recs[k][r] = parts_of[u][k * BLK : (k + 1) * BLK] + recs[k][at("prev_rec", r, k)]
            summed = jnp.sum(parts_of[u][KW * BLK :], axis=1, keepdims=True)
            total = total + jnp.where(lanes == at("link", r), summed, 0.0)
        return total

    def start_rows(base, count, total):
        news = [jnp.where(base + u < at("count", 0), lam[base + u], 0.0) for u in range(count)]
        for u in range(count):
            lam[base + u] = news[u]
        return chain_rows(base, count, [new.astype(BF16) for new in news], total)

    def next_rows(more):
        def step(base, count, state):
            total, demand = state
            news = []
            for u in range(count):
                r = base + u
                gathered = [bar[at("pattern", r, k)] for k in range(KW)] + [first_wide[at("link", r)]]
                coupled = jnp.dot(coupling[r], jnp.concatenate(gathered, axis=0), preferred_element_type=F32)
                target = spread(demand, u) + wind[r].astype(F32)
                new = lam[r] + dual_step * (target - coupled)
                news.append(jnp.where(r < at("count", 0), new, 0.0))
            for u in range(count):
                lam[base + u] = news[u]
            if more:
                total = chain_rows(base, count, [new.astype(BF16) for new in news], total)
            return total, pltpu.roll(demand, demand.shape[1] - count, 1)

        return loop(rows, step, (zero, demand_wide[...]))[0]

    def send_first_sum(iteration, total):
        send_first[iteration] = (total / scen_total).astype(BF16)
        for by in range(1, scens):
            first_copy(iteration, by).start()

    def move_first(iteration):
        total = send_first[iteration].astype(F32)
        for by in range(1, scens):
            first_copy(iteration, by).wait()
            total = total + got_first[iteration, by].astype(F32)
        now = first_t[...]
        new = jnp.clip(now - first_step * (commit_cost_t[...] - total), 0.0, 1.0)
        first_t[...] = new
        extrapolated = 2.0 * new - now

        def step(base, count, columns):
            for u in range(count):
                first_wide[base + u] = spread(columns, u).astype(BF16)
            return pltpu.roll(columns, columns.shape[1] - count, 1)

        loop(blocks, step, extrapolated)

    def gather_local(base, count, cost):
        moved = []
        for u in range(count):
            b = base + u
            grad = own[at("last_own", b)]
            for k in range(KW):
                grad = grad + recs[k][at("last_rec", b, k)]
            moved.append(second[b] - primal_step * (spread(cost, u) - grad))
        for u in range(count):
            outs[base + u] = moved[u]
        return pltpu.roll(cost, cost.shape[1] - count, 1)

    def answer_terms(iteration):
        def chunk(c, carry):
            @pl.when(has_prev)
            def _():
                terms_copy(iteration, c).wait_recv()

                def step(base, count, inner):
                    bars = []
                    for u in range(count):
                        d = c * span + base + u
                        b = at("block_of_slot", d)
                        new = jnp.maximum(outs[b] + primal_step * got_terms[iteration][1 + d].astype(F32), 0.0)
                        bars.append((2.0 * new - second[b]).astype(BF16))
                    for u in range(count):
                        send_bar[c * span + base + u] = bars[u]
                    return inner

                loop(span, step)
                bar_copy(iteration, c).start()

            return carry

        lax.fori_loop(0, CHUNKS, chunk, 0)

    def move_second(iteration):
        def step(base, count, carry):
            news = []
            for u in range(count):
                b = base + u
                terms = got_terms[iteration][at("slot_of_block", b)].astype(F32)
                new = jnp.maximum(outs[b] + primal_step * terms, 0.0)
                news.append((new, (2.0 * new - second[b]).astype(BF16)))
            for u in range(count):
                second[base + u], bar[base + u] = news[u]
            return carry

        loop(blocks, step)

    def finish_sends(copy, iteration):
        def chunk(c, carry):
            copy(iteration, c).wait_send()
            return carry

        lax.fori_loop(0, CHUNKS, chunk, 0)

    def finish_receives(copy, iteration):
        def chunk(c, carry):
            copy(iteration, c).wait_recv()
            return carry

        lax.fori_loop(0, CHUNKS, chunk, 0)

    loads[0].wait()
    loads[1].wait()
    loop(ties, start_ties)
    send_all_terms(0)
    loads[2].wait()
    loads[3].wait()
    total = loop(rows, start_rows, zero)
    send_first_sum(0, total)
    loads[4].wait()
    for iteration in range(ITERS):
        more = iteration < ITERS - 1
        loop(blocks, gather_local, cost_t[...])
        answer_terms(iteration)
        move_second(iteration)
        move_first(iteration)
        if iteration == 0:
            loads[5].wait()
        if not more:
            commit_out[...] = first_t[...]
            store_second = pltpu.make_async_copy(second, second_out, store_sems.at[0])
            store_second.start()
        total = next_rows(more)
        if more:
            send_first_sum(iteration + 1, total)
        else:
            store_lam = pltpu.make_async_copy(lam, lam_out, store_sems.at[1])
            store_lam.start()

        @pl.when(has_next)
        def _():
            finish_sends(terms_copy, iteration)
            finish_receives(bar_copy, iteration)

        next_ties(iteration, more)
        if more:
            send_all_terms(iteration + 1)

        @pl.when(has_prev)
        def _():
            finish_sends(bar_copy, iteration)

    store_mu = pltpu.make_async_copy(mu, mu_out, store_sems.at[2])
    store_mu.start()
    store_second.wait()
    store_lam.wait()
    store_mu.wait()


def body(
    coupling,
    tie_blocks,
    w_pattern,
    link_pattern,
    left_bounds,
    right_bounds,
    block_counts,
    commit_cost,
    dispatch_cost,
    demand,
    wind_error,
    commit_start,
    dispatch_start,
    dual_start,
    tie_start,
):
    parts, scens = lax.axis_size("net"), lax.axis_size("scen")
    blocks = dispatch_start.shape[0]
    block_shape = dispatch_start.shape[1:]
    few = blocks * 3 // 4
    vmem = pl.BlockSpec(memory_space=pltpu.VMEM)
    smem = pl.BlockSpec(memory_space=pltpu.SMEM)
    anywhere = pl.BlockSpec(memory_space=pl.ANY)
    sems = pltpu.SemaphoreType.DMA
    table, most = pl.pallas_call(
        functools.partial(prepare, few),
        out_shape=(
            jax.ShapeDtypeStruct((TABLE_ROWS, blocks), jnp.int32),
            jax.ShapeDtypeStruct((1, blocks), jnp.int32),
        ),
        in_specs=[vmem] * 4 + [smem],
        out_specs=(vmem, vmem),
        scratch_shapes=[
            pltpu.VMEM((8, blocks), jnp.int32),
            pltpu.VMEM((1, blocks), jnp.int32),
            pltpu.VMEM((parts, 8, blocks), jnp.int32),
            sems((parts,)),
            sems((parts,)),
        ],
        compiler_params=pltpu.CompilerParams(collective_id=0, has_side_effects=True),
    )(left_bounds[None], right_bounds[None], w_pattern.T, link_pattern[None], block_counts)

    def call(slots, collective_id, operands):
        wide = lambda count, kind: pltpu.VMEM((count,) + block_shape, kind)
        rows, ties = dual_start.shape[0], tie_start.shape[0]
        return pl.pallas_call(
            kernel,
            out_shape=(
                jax.ShapeDtypeStruct((BLK, blocks), F32),
                jax.ShapeDtypeStruct(dispatch_start.shape, F32),
                jax.ShapeDtypeStruct(dual_start.shape, F32),
                jax.ShapeDtypeStruct(tie_start.shape, F32),
            ),
            in_specs=[smem] + [vmem] * 4 + [anywhere] * 6,
            out_specs=(vmem, anywhere, anywhere, anywhere),
            scratch_shapes=[
                pltpu.VMEM(coupling.shape, BF16),
                pltpu.VMEM(tie_blocks.shape, BF16),
                pltpu.VMEM(wind_error.shape, BF16),
                wide(blocks, F32),
                wide(rows, F32),
                wide(ties, F32),
                wide(rows + 1, F32),
                wide(rows + 1, F32),
                wide(rows + 1, F32),
                wide(rows + 1, F32),
                wide(ties + 1, F32),
                wide(ties + 1, F32),
                wide(slots, BF16),
                wide(slots + 1, BF16),
                wide(slots + 1, BF16),
                wide(slots, BF16),
                wide(slots, BF16),
                wide(slots, BF16),
                wide(blocks, BF16),
                wide(blocks, BF16),
                pltpu.VMEM(block_shape, F32),
                pltpu.VMEM(block_shape, F32),
                pltpu.VMEM((ITERS,) + block_shape, BF16),
                pltpu.VMEM((ITERS, scens) + block_shape, BF16),
                sems((6,)),
                sems((3,)),
                sems((ITERS, CHUNKS)),
                sems((ITERS, CHUNKS)),
                sems((ITERS, CHUNKS)),
                sems((ITERS, CHUNKS)),
                sems((ITERS, scens)),
                sems((ITERS, scens)),
            ],
            compiler_params=pltpu.CompilerParams(
                collective_id=collective_id, has_side_effects=True, vmem_limit_bytes=62 * 2**20
            ),
            cost_estimate=pl.CostEstimate(flops=32 * 10**8, bytes_accessed=30 * 10**6, transcendentals=0),
        )(*operands)

    operands = (
        table,
        dispatch_cost.T,
        demand.T,
        commit_cost.T,
        commit_start.T,
        coupling,
        tie_blocks,
        wind_error,
        dispatch_start,
        dual_start,
        tie_start,
    )
    commit_t, second, lam, mu = lax.cond(
        most[0, 0] > 0,
        lambda *given: call(blocks, 1, given),
        lambda *given: call(few, 2, given),
        *operands,
    )
    return commit_t.T, second, lam, mu


def solution(mesh):
    return jax.shard_map(
        body,
        mesh=mesh,
        in_specs=(
            P("net", None, None),
            P("net", None, None),
            P("net", None),
            P("net"),
            P("net"),
            P("net"),
            P("net"),
            P("net", None),
            P("net", None),
            P("net", None),
            P("net", None, "scen"),
            P("net", None),
            P("net", None, "scen"),
            P("net", None, "scen"),
            P("net", None, "scen"),
        ),
        out_specs=(
            P("net", None),
            P("net", None, "scen"),
            P("net", None, "scen"),
            P("net", None, "scen"),
        ),
        check_vma=False,
    )
```

```python
import functools

import jax
import jax.numpy as jnp
from jax import lax
from jax.experimental import pallas as pl
from jax.experimental.pallas import tpu as pltpu
from jax.sharding import PartitionSpec as P

BLK = 64
KW = 4
ITERS = 2
CHUNKS = 8
UNROLL = 16
RELAYED = 8

primal_step = 0.4
first_step = 1.0
dual_step = 0.4

F32 = jnp.float32
BF16 = jnp.bfloat16
MESH = pl.DeviceIdType.MESH


def transposed_dot(a, b):
    return lax.dot_general(a, b, (((0,), (0,)), ((), ())), preferred_element_type=F32)


def spread(columns, at):
    return jnp.broadcast_to(columns[:, at : at + 1], columns.shape)


def loop(count, step, carry=0, unroll=UNROLL):
    unroll = max(u for u in range(1, unroll + 1) if count % u == 0)
    return lax.fori_loop(0, count // unroll, lambda c, state: step(c * unroll, unroll, state), carry)


TABLE = dict(
    pattern=0,
    link=4,
    prev_rec=5,
    last_rec=9,
    right=13,
    prev_own=14,
    last_own=15,
    prev_out=16,
    last_out=17,
    slot_of_tie=18,
    slot_of_block=19,
    block_of_slot=20,
    most=21,
    count=22,
)
TABLE_ROWS = 24


def prepare(slots_few, left, right, pattern, link, count, table, most, message, padded, inbox, send_sems, recv_sems):
    me_s, me = lax.axis_index("scen"), lax.axis_index("net")
    parts = lax.axis_size("net")
    lanes = table.shape[1]
    blocks = lanes

    entry = pltpu.get_barrier_semaphore()
    for by in range(1, parts):
        pl.semaphore_signal(entry, inc=1, device_id=(me_s, lax.rem(me + by, parts)), device_id_type=MESH)

    down = lax.broadcasted_iota(jnp.int32, (lanes, lanes), 0)
    along = lax.broadcasted_iota(jnp.int32, (lanes, lanes), 1)

    def both(row):
        spread_row = jnp.broadcast_to(row, (lanes, lanes)).astype(F32)
        return spread_row, spread_row.T

    def most_of(mask, values):
        return jnp.max(jnp.where(mask, values.astype(F32), -1.0), axis=0, keepdims=True)

    def or_else(found, other):
        return jnp.where(found < 0.0, jnp.float32(other), found).astype(jnp.int32)

    def chain(row, n):
        at_lane, at_row = both(row)
        previous = most_of((at_lane == at_row) & (down < along) & (down < n), down)
        last = most_of((at_row == along.astype(F32)) & (down < n), down)
        return previous, last

    def slots_of(row):
        at_lane, at_row = both(row)
        hit = at_row == along.astype(F32)
        present = jnp.max(jnp.where(hit, 1.0, 0.0), axis=0, keepdims=True)
        present_wide = jnp.broadcast_to(present, (lanes, lanes))
        present_down = present_wide.T
        before = jnp.sum(jnp.where(down < along, present_down, 0.0), axis=0, keepdims=True)
        _, before_down = both(before)
        chosen = (present_down > 0.0) & (before_down == along.astype(F32))
        block_of_slot = most_of(chosen, down)
        return present, before, block_of_slot, jnp.sum(present, axis=1, keepdims=True)

    present, before, block_of_slot, count_of = slots_of(left[...])
    message[...] = jnp.zeros(message.shape, jnp.int32)
    message[0:1] = left[...]
    counted = jnp.broadcast_to(count_of, (1, lanes)).astype(jnp.int32)
    message[1:2] = jnp.where(me > 0, counted, 0)
    pl.semaphore_wait(entry, parts - 1)

    def copy(by):
        return pltpu.make_async_remote_copy(
            src_ref=message,
            dst_ref=inbox.at[by],
            send_sem=send_sems.at[by],
            recv_sem=recv_sems.at[by],
            device_id=(me_s, lax.rem(me + by, parts)),
            device_id_type=MESH,
        )

    for by in range(1, parts):
        copy(by).start()

    rows, ties = pattern.shape[1], right.shape[1]
    table[...] = jnp.zeros(table.shape, jnp.int32)
    sentinel = jnp.zeros((1, lanes), jnp.int32) + lanes
    for k in range(KW):
        padded[...] = sentinel
        padded[:, 0:rows] = pattern[k : k + 1]
        row = padded[...]
        table[TABLE["pattern"] + k : TABLE["pattern"] + k + 1] = row
        previous, last = chain(row, rows)
        table[TABLE["prev_rec"] + k : TABLE["prev_rec"] + k + 1] = or_else(previous, rows)
        table[TABLE["last_rec"] + k : TABLE["last_rec"] + k + 1] = or_else(last, rows)
    table[TABLE["link"] : TABLE["link"] + 1, 0:rows] = link[...]
    previous, last = chain(right[...], ties)
    table[TABLE["right"] : TABLE["right"] + 1] = right[...]
    table[TABLE["prev_own"] : TABLE["prev_own"] + 1] = or_else(previous, ties)
    table[TABLE["last_own"] : TABLE["last_own"] + 1] = or_else(last, ties)
    table[TABLE["slot_of_block"] : TABLE["slot_of_block"] + 1] = jnp.where(present > 0.0, before + 1.0, 0.0).astype(jnp.int32)
    table[TABLE["block_of_slot"] : TABLE["block_of_slot"] + 1] = or_else(block_of_slot, 0)
    table[TABLE["count"] : TABLE["count"] + 1] = jnp.zeros((1, lanes), jnp.int32) + count[0]

    highest = message[1:2]
    for by in range(1, parts):
        copy(by).wait()
        highest = jnp.maximum(highest, inbox[by, 1:2])
    most[...] = jnp.where(highest > slots_few, 1, 0)
    left_next = inbox[parts - 1, 0:1]
    previous, last = chain(left_next, ties)
    present, before, block_of_slot, _ = slots_of(left_next)
    at_lane, at_row = both(left_next)
    _, last_down = both(last)
    _, before_down = both(before)
    slot_of_tie = most_of(at_lane == down.astype(F32), before_down)
    _, block_down = both(block_of_slot)
    block_lane, _ = both(block_of_slot)
    last_out = most_of(block_lane == down.astype(F32), last_down)
    table[TABLE["prev_out"] : TABLE["prev_out"] + 1] = or_else(previous, ties)
    table[TABLE["last_out"] : TABLE["last_out"] + 1] = or_else(last_out, ties)
    table[TABLE["slot_of_tie"] : TABLE["slot_of_tie"] + 1] = slot_of_tie.astype(jnp.int32)


def kernel(
    index,
    cost_t,
    demand_t,
    commit_cost_t,
    commit_t,
    coupling_hbm,
    tie_hbm,
    wind_hbm,
    second_hbm,
    lam_hbm,
    mu_hbm,
    commit_out,
    second_out,
    lam_out,
    mu_out,
    coupling,
    tie,
    wind,
    second,
    lam,
    mu,
    rec0,
    rec1,
    rec2,
    rec3,
    outs,
    own,
    send_terms,
    got_terms0,
    got_terms1,
    send_bar,
    got_bar0,
    got_bar1,
    relay0,
    relay1,
    bar,
    first_wide,
    first_t,
    demand_wide,
    send_first,
    got_first,
    load_sems,
    store_sems,
    terms_ssem,
    terms_rsem,
    bar_ssem,
    bar_rsem,
    relay_ssem,
    relay_rsem,
    first_ssem,
    first_rsem,
):
    recs = (rec0, rec1, rec2, rec3)
    got_terms, got_bar, relay = (got_terms0, got_terms1), (got_bar0, got_bar1), (relay0, relay1)
    me_s, me = lax.axis_index("scen"), lax.axis_index("net")
    scens, parts = lax.axis_size("scen"), lax.axis_size("net")
    rows, ties, blocks = lam.shape[0], mu.shape[0], second.shape[0]
    slots = send_terms.shape[0]
    scen_total = lam.shape[2] * scens
    has_next, has_prev = me < parts - 1, me > 0
    relayed = parts == RELAYED
    low, high = parts // 2 - 1, parts // 2
    is_low, is_high, is_first, is_last = me == low, me == high, me == 0, me == parts - 1

    def at(name, i, k=0):
        return index[TABLE[name] + k, i]

    loads = [
        pltpu.make_async_copy(src, dst, load_sems.at[i])
        for i, (src, dst) in enumerate(
            [(tie_hbm, tie), (mu_hbm, mu), (coupling_hbm, coupling), (lam_hbm, lam), (second_hbm, second), (wind_hbm, wind)]
        )
    ]
    for copy in loads:
        copy.start()

    entry = pltpu.get_barrier_semaphore()
    for by in range(1, scens):
        pl.semaphore_signal(entry, inc=1, device_id=(lax.rem(me_s + by, scens), me), device_id_type=MESH)

    @pl.when(has_next)
    def _():
        pl.semaphore_signal(entry, inc=1, device_id=(me_s, me + 1), device_id_type=MESH)

    @pl.when(has_prev)
    def _():
        pl.semaphore_signal(entry, inc=1, device_id=(me_s, me - 1), device_id_type=MESH)

    greeted = scens - 1 + has_next.astype(jnp.int32) + has_prev.astype(jnp.int32)
    if relayed:
        for mine, others in ((0, (low, high)), (parts - 1, (low, high)), (low, (0, parts - 1)), (high, (0, parts - 1))):

            @pl.when(me == mine)
            def _(others=others):
                for other in others:
                    pl.semaphore_signal(entry, inc=1, device_id=(me_s, jnp.int32(other)), device_id_type=MESH)

            greeted = greeted + 2 * (me == mine).astype(jnp.int32)

    zero = jnp.zeros(second.shape[1:], F32)
    for ref in recs:
        ref[rows] = zero
    outs[ties] = zero
    own[ties] = zero
    for iteration in range(ITERS):
        got_terms[iteration][0] = zero.astype(BF16)
    first_t[...] = commit_t[...]
    demand_wide[:, 0:rows] = demand_t[...]

    @pl.when(jnp.logical_not(has_prev))
    def _():
        for iteration in range(ITERS):
            got_terms[iteration][pl.ds(1, slots)] = jnp.zeros((slots,) + second.shape[1:], BF16)

    @pl.when(jnp.logical_not(has_next))
    def _():
        for iteration in range(ITERS):
            got_bar[iteration][...] = jnp.zeros((slots,) + second.shape[1:], BF16)

    pl.semaphore_wait(entry, greeted)

    lanes = lax.broadcasted_iota(jnp.int32, second.shape[1:], 1)
    span = slots // CHUNKS

    def terms_copy(iteration, c):
        return pltpu.make_async_remote_copy(
            src_ref=send_terms.at[pl.ds(c * span, span)],
            dst_ref=got_terms[iteration].at[pl.ds(1 + c * span, span)],
            send_sem=terms_ssem.at[iteration, c],
            recv_sem=terms_rsem.at[iteration, c],
            device_id=(me_s, me + 1),
            device_id_type=MESH,
        )

    def bar_copy(iteration, c):
        return pltpu.make_async_remote_copy(
            src_ref=send_bar.at[pl.ds(c * span, span)],
            dst_ref=got_bar[iteration].at[pl.ds(c * span, span)],
            send_sem=bar_ssem.at[iteration, c],
            recv_sem=bar_rsem.at[iteration, c],
            device_id=(me_s, me - 1),
            device_id_type=MESH,
        )

    def to_relay(iteration, c, source, send_sem, device):
        return pltpu.make_async_remote_copy(
            src_ref=source.at[pl.ds(c * span, span)],
            dst_ref=relay[iteration].at[pl.ds(c // 2 * span, span)],
            send_sem=send_sem.at[iteration, c],
            recv_sem=relay_rsem.at[iteration, c],
            device_id=(me_s, jnp.int32(device)),
            device_id_type=MESH,
        )

    def from_relay(iteration, c, target, shift, recv_sem, device):
        return pltpu.make_async_remote_copy(
            src_ref=relay[iteration].at[pl.ds(c // 2 * span, span)],
            dst_ref=target[iteration].at[pl.ds(shift + c * span, span)],
            send_sem=relay_ssem.at[iteration, c],
            recv_sem=recv_sem.at[iteration, c],
            device_id=(me_s, jnp.int32(device)),
            device_id_type=MESH,
        )

    def terms_relay(iteration, c):
        return to_relay(iteration, c, send_terms, terms_ssem, parts - 1)

    def terms_onward(iteration, c):
        return from_relay(iteration, c, got_terms, 1, terms_rsem, high)

    def bar_relay(iteration, c):
        return to_relay(iteration, c, send_bar, bar_ssem, 0)

    def bar_onward(iteration, c):
        return from_relay(iteration, c, got_bar, 0, bar_rsem, low)

    def start_split(iteration, c, sender, direct, relay_of):
        if not relayed:
            direct(iteration, c).start()
            return
        by_relay = sender & (lax.rem(c, 2) == 1)

        @pl.when(by_relay)
        def _():
            relay_of(iteration, c).start()

        @pl.when(jnp.logical_not(by_relay))
        def _():
            direct(iteration, c).start()

    def pass_on(iteration, arriving, onward):
        def step(h, carry):
            arriving(iteration, 2 * h + 1).wait_recv()
            onward(iteration, 2 * h + 1).start()
            return carry

        lax.fori_loop(0, CHUNKS // 2, step, 0)

    def finish_onward(iteration, onward):
        def step(h, carry):
            onward(iteration, 2 * h + 1).wait_send()
            return carry

        lax.fori_loop(0, CHUNKS // 2, step, 0)

    def first_copy(iteration, by):
        return pltpu.make_async_remote_copy(
            src_ref=send_first.at[iteration],
            dst_ref=got_first.at[iteration, by],
            send_sem=first_ssem.at[iteration, by],
            recv_sem=first_rsem.at[iteration, by],
            device_id=(lax.rem(me_s + by, scens), me),
            device_id_type=MESH,
        )

    def chain_ties(base, count, news):
        parts_of = [transposed_dot(tie[base + u], news[u].astype(BF16)) for u in range(count)]
        for u in range(count):
            j = base + u
            own[j] = parts_of[u][:BLK] + own[at("prev_own", j)]
            outs[j] = parts_of[u][BLK:] + outs[at("prev_out", j)]

    def start_ties(base, count, carry):
        news = [jnp.where(has_next, mu[base + u], 0.0) for u in range(count)]
        for u in range(count):
            mu[base + u] = news[u]
        chain_ties(base, count, news)
        return carry

    def next_ties(iteration, more):
        def step(base, count, carry):
            news = []
            for u in range(count):
                j = base + u
                stacked = jnp.concatenate([bar[at("right", j)], got_bar[iteration][at("slot_of_tie", j)]], axis=0)
                product = jnp.dot(tie[j], stacked, preferred_element_type=F32)
                news.append(jnp.where(has_next, mu[j] - dual_step * product, 0.0))
            for u in range(count):
                mu[base + u] = news[u]
            if more:
                chain_ties(base, count, news)
            return carry

        loop(ties, step)

    def send_all_terms(iteration):
        def chunk(c, carry):
            def step(base, count, inner):
                blocks_of = [outs[at("last_out", c * span + base + u)] for u in range(count)]
                for u in range(count):
                    send_terms[c * span + base + u] = blocks_of[u].astype(BF16)
                return inner

            loop(span, step)

            @pl.when(has_next)
            def _():
                start_split(iteration, c, is_low, terms_copy, terms_relay)

            return carry

        lax.fori_loop(0, CHUNKS, chunk, 0)
        if relayed:

            @pl.when(is_last)
            def _():
                pass_on(iteration, terms_relay, terms_onward)

    def chain_rows(base, count, halves, total):
        parts_of = [transposed_dot(coupling[base + u], halves[u]) for u in range(count)]
        for u in range(count):
            r = base + u
            for k in range(KW):
                recs[k][r] = parts_of[u][k * BLK : (k + 1) * BLK] + recs[k][at("prev_rec", r, k)]
            summed = jnp.sum(parts_of[u][KW * BLK :], axis=1, keepdims=True)
            total = total + jnp.where(lanes == at("link", r), summed, 0.0)
        return total

    def start_rows(base, count, total):
        news = [jnp.where(base + u < at("count", 0), lam[base + u], 0.0) for u in range(count)]
        for u in range(count):
            lam[base + u] = news[u]
        return chain_rows(base, count, [new.astype(BF16) for new in news], total)

    def next_rows(more):
        def step(base, count, state):
            total, demand = state
            news = []
            for u in range(count):
                r = base + u
                gathered = [bar[at("pattern", r, k)] for k in range(KW)] + [first_wide[at("link", r)]]
                coupled = jnp.dot(coupling[r], jnp.concatenate(gathered, axis=0), preferred_element_type=F32)
                target = spread(demand, u) + wind[r].astype(F32)
                new = lam[r] + dual_step * (target - coupled)
                news.append(jnp.where(r < at("count", 0), new, 0.0))
            for u in range(count):
                lam[base + u] = news[u]
            if more:
                total = chain_rows(base, count, [new.astype(BF16) for new in news], total)
            return total, pltpu.roll(demand, demand.shape[1] - count, 1)

        return loop(rows, step, (zero, demand_wide[...]))[0]

    def send_first_sum(iteration, total):
        send_first[iteration] = (total / scen_total).astype(BF16)
        for by in range(1, scens):
            first_copy(iteration, by).start()

    def move_first(iteration):
        total = send_first[iteration].astype(F32)
        for by in range(1, scens):
            first_copy(iteration, by).wait()
            total = total + got_first[iteration, by].astype(F32)
        now = first_t[...]
        new = jnp.clip(now - first_step * (commit_cost_t[...] - total), 0.0, 1.0)
        first_t[...] = new
        extrapolated = 2.0 * new - now

        def step(base, count, columns):
            for u in range(count):
                first_wide[base + u] = spread(columns, u).astype(BF16)
            return pltpu.roll(columns, columns.shape[1] - count, 1)

        loop(blocks, step, extrapolated)

    def gather_local(base, count, cost):
        moved = []
        for u in range(count):
            b = base + u
            grad = own[at("last_own", b)]
            for k in range(KW):
                grad = grad + recs[k][at("last_rec", b, k)]
            moved.append(second[b] - primal_step * (spread(cost, u) - grad))
        for u in range(count):
            outs[base + u] = moved[u]
        return pltpu.roll(cost, cost.shape[1] - count, 1)

    def answer_terms(iteration):
        def chunk(c, carry):
            @pl.when(has_prev)
            def _():
                terms_copy(iteration, c).wait_recv()

                def step(base, count, inner):
                    bars = []
                    for u in range(count):
                        d = c * span + base + u
                        b = at("block_of_slot", d)
                        new = jnp.maximum(outs[b] + primal_step * got_terms[iteration][1 + d].astype(F32), 0.0)
                        bars.append((2.0 * new - second[b]).astype(BF16))
                    for u in range(count):
                        send_bar[c * span + base + u] = bars[u]
                    return inner

                loop(span, step)
                start_split(iteration, c, is_high, bar_copy, bar_relay)

            return carry

        lax.fori_loop(0, CHUNKS, chunk, 0)

    def move_second(iteration):
        def step(base, count, carry):
            news = []
            for u in range(count):
                b = base + u
                terms = got_terms[iteration][at("slot_of_block", b)].astype(F32)
                new = jnp.maximum(outs[b] + primal_step * terms, 0.0)
                news.append((new, (2.0 * new - second[b]).astype(BF16)))
            for u in range(count):
                second[base + u], bar[base + u] = news[u]
            return carry

        loop(blocks, step)

    def finish_sends(copy, iteration):
        def chunk(c, carry):
            copy(iteration, c).wait_send()
            return carry

        lax.fori_loop(0, CHUNKS, chunk, 0)

    def finish_receives(copy, iteration):
        def chunk(c, carry):
            copy(iteration, c).wait_recv()
            return carry

        lax.fori_loop(0, CHUNKS, chunk, 0)

    loads[0].wait()
    loads[1].wait()
    loop(ties, start_ties)
    send_all_terms(0)
    loads[2].wait()
    loads[3].wait()
    total = loop(rows, start_rows, zero)
    send_first_sum(0, total)
    loads[4].wait()
    for iteration in range(ITERS):
        more = iteration < ITERS - 1
        loop(blocks, gather_local, cost_t[...])
        answer_terms(iteration)
        if relayed:

            @pl.when(is_first)
            def _():
                pass_on(iteration, bar_relay, bar_onward)

        move_second(iteration)
        move_first(iteration)
        if iteration == 0:
            loads[5].wait()
        if not more:
            commit_out[...] = first_t[...]
            store_second = pltpu.make_async_copy(second, second_out, store_sems.at[0])
            store_second.start()
        total = next_rows(more)
        if more:
            send_first_sum(iteration + 1, total)
        else:
            store_lam = pltpu.make_async_copy(lam, lam_out, store_sems.at[1])
            store_lam.start()

        @pl.when(has_next)
        def _():
            finish_sends(terms_copy, iteration)
            finish_receives(bar_copy, iteration)

        next_ties(iteration, more)
        if more:
            send_all_terms(iteration + 1)

        @pl.when(has_prev)
        def _():
            finish_sends(bar_copy, iteration)

        if relayed:

            @pl.when(is_last)
            def _():
                finish_onward(iteration, terms_onward)

            @pl.when(is_first)
            def _():
                finish_onward(iteration, bar_onward)

    store_mu = pltpu.make_async_copy(mu, mu_out, store_sems.at[2])
    store_mu.start()
    store_second.wait()
    store_lam.wait()
    store_mu.wait()


def body(
    coupling,
    tie_blocks,
    w_pattern,
    link_pattern,
    left_bounds,
    right_bounds,
    block_counts,
    commit_cost,
    dispatch_cost,
    demand,
    wind_error,
    commit_start,
    dispatch_start,
    dual_start,
    tie_start,
):
    parts, scens = lax.axis_size("net"), lax.axis_size("scen")
    blocks = dispatch_start.shape[0]
    block_shape = dispatch_start.shape[1:]
    few = blocks * 3 // 4
    vmem = pl.BlockSpec(memory_space=pltpu.VMEM)
    smem = pl.BlockSpec(memory_space=pltpu.SMEM)
    anywhere = pl.BlockSpec(memory_space=pl.ANY)
    sems = pltpu.SemaphoreType.DMA
    table, most = pl.pallas_call(
        functools.partial(prepare, few),
        out_shape=(
            jax.ShapeDtypeStruct((TABLE_ROWS, blocks), jnp.int32),
            jax.ShapeDtypeStruct((1, blocks), jnp.int32),
        ),
        in_specs=[vmem] * 4 + [smem],
        out_specs=(vmem, vmem),
        scratch_shapes=[
            pltpu.VMEM((8, blocks), jnp.int32),
            pltpu.VMEM((1, blocks), jnp.int32),
            pltpu.VMEM((parts, 8, blocks), jnp.int32),
            sems((parts,)),
            sems((parts,)),
        ],
        compiler_params=pltpu.CompilerParams(collective_id=0, has_side_effects=True),
    )(left_bounds[None], right_bounds[None], w_pattern.T, link_pattern[None], block_counts)

    def call(slots, collective_id, operands):
        wide = lambda count, kind: pltpu.VMEM((count,) + block_shape, kind)
        rows, ties = dual_start.shape[0], tie_start.shape[0]
        return pl.pallas_call(
            kernel,
            out_shape=(
                jax.ShapeDtypeStruct((BLK, blocks), F32),
                jax.ShapeDtypeStruct(dispatch_start.shape, F32),
                jax.ShapeDtypeStruct(dual_start.shape, F32),
                jax.ShapeDtypeStruct(tie_start.shape, F32),
            ),
            in_specs=[smem] + [vmem] * 4 + [anywhere] * 6,
            out_specs=(vmem, anywhere, anywhere, anywhere),
            scratch_shapes=[
                pltpu.VMEM(coupling.shape, BF16),
                pltpu.VMEM(tie_blocks.shape, BF16),
                pltpu.VMEM(wind_error.shape, BF16),
                wide(blocks, F32),
                wide(rows, F32),
                wide(ties, F32),
                wide(rows + 1, F32),
                wide(rows + 1, F32),
                wide(rows + 1, F32),
                wide(rows + 1, F32),
                wide(ties + 1, F32),
                wide(ties + 1, F32),
                wide(slots, BF16),
                wide(slots + 1, BF16),
                wide(slots + 1, BF16),
                wide(slots, BF16),
                wide(slots, BF16),
                wide(slots, BF16),
                wide(slots // 2, BF16),
                wide(slots // 2, BF16),
                wide(blocks, BF16),
                wide(blocks, BF16),
                pltpu.VMEM(block_shape, F32),
                pltpu.VMEM(block_shape, F32),
                pltpu.VMEM((ITERS,) + block_shape, BF16),
                pltpu.VMEM((ITERS, scens) + block_shape, BF16),
                sems((6,)),
                sems((3,)),
                sems((ITERS, CHUNKS)),
                sems((ITERS, CHUNKS)),
                sems((ITERS, CHUNKS)),
                sems((ITERS, CHUNKS)),
                sems((ITERS, CHUNKS)),
                sems((ITERS, CHUNKS)),
                sems((ITERS, scens)),
                sems((ITERS, scens)),
            ],
            compiler_params=pltpu.CompilerParams(
                collective_id=collective_id, has_side_effects=True, vmem_limit_bytes=62 * 2**20
            ),
            cost_estimate=pl.CostEstimate(flops=32 * 10**8, bytes_accessed=30 * 10**6, transcendentals=0),
        )(*operands)

    operands = (
        table,
        dispatch_cost.T,
        demand.T,
        commit_cost.T,
        commit_start.T,
        coupling,
        tie_blocks,
        wind_error,
        dispatch_start,
        dual_start,
        tie_start,
    )
    commit_t, second, lam, mu = lax.cond(
        most[0, 0] > 0,
        lambda *given: call(blocks, 1, given),
        lambda *given: call(few, 2, given),
        *operands,
    )
    return commit_t.T, second, lam, mu


def solution(mesh):
    return jax.shard_map(
        body,
        mesh=mesh,
        in_specs=(
            P("net", None, None),
            P("net", None, None),
            P("net", None),
            P("net"),
            P("net"),
            P("net"),
            P("net"),
            P("net", None),
            P("net", None),
            P("net", None),
            P("net", None, "scen"),
            P("net", None),
            P("net", None, "scen"),
            P("net", None, "scen"),
            P("net", None, "scen"),
        ),
        out_specs=(
            P("net", None),
            P("net", None, "scen"),
            P("net", None, "scen"),
            P("net", None, "scen"),
        ),
        check_vma=False,
    )
```
